32 devices in a mesh: dp: 4 (over x, core), seq: 8 (over z, y).
Axes of the slice: x: 2, y: 2, z: 4, core: 2. Of those that a mesh axis runs over, the one named last changes fastest.
Arguments:
- pipe_field: bfloat16 [4, 16384, 256], P('dp', 'seq'), may hold values from -6 to 6
- conv_weight: bfloat16 [3, 3, 256, 256], replicated, may hold values from -0.21875 to 0.21875
- conv_bias: float32 [3, 256], replicated, may hold values from -3 to 3
- norm_gain: float32 [256], replicated, may hold values from 0.1 to 1.9
- query_weight: bfloat16 [256, 256], replicated, may hold values from -0.18875 to 0.18875
- key_weight: bfloat16 [256, 256], replicated, may hold values from -5.6875 to 5.6875
- value_weight: bfloat16 [256, 256], replicated, may hold values from -0.375 to 0.375
- out_weight: bfloat16 [256, 256], replicated, may hold values from -0.375 to 0.375
- upstream: bfloat16 [4, 16384, 256], P('dp', 'seq'), may hold values from -0.0234375 to 0.0234375
Outputs:
- attended: float32 [4, 2048, 256], P('dp', 'seq')
- weight_grad: float32 [3, 3, 256, 256], replicated
- bias_grad: float32 [3, 256], replicated
The draws below stay inside these ranges and needn't reach their ends.
All inputs are finite; a program needn't handle non-finite values.
Results may differ from the reference program's by a relative error of at most 0.03.
Values may be sent and summed in bfloat16 or wider, within the bound.
A program may use at most 128 MiB of HBM per device.

```python
import jax
import jax.numpy as jnp
from jax import lax

C = 256
HEADS = 4
LAYERS = 3
FIRST_SPACING = 2048
SECOND_SPACING = 4096
THIRD_SPACING = 8192
POOL = 8
RUNS = 4
CELLS = 16384


def shared_base(key):
    return jax.random.uniform(key, (C, C), jnp.float32, -3.0, 3.0)


def draw_query_weight(key, part):
    base = shared_base(key)
    return (base * C ** (-0.5)).astype(jnp.bfloat16)


def draw_key_weight(key, part):
    key = jax.random.fold_in(key, 5)
    fresh = jax.random.uniform(key, (C, C), jnp.float32, -3.0, 3.0)
    return (fresh * C ** (-0.5)).astype(jnp.bfloat16)


def block_levels(rng, shape, split, least, largest):
    loudness = 1.0
    for axis_at, shards_of in split:
        draws = jax.random.uniform(jax.random.fold_in(jax.random.fold_in(rng, 6), axis_at), (shards_of,), jnp.float32, least / len(split), largest / len(split))
        loudness = loudness * jnp.repeat(jnp.exp(draws), shape[axis_at] // shards_of).reshape((-1,) + (1,) * (len(shape) - 1 - axis_at))
    return loudness


def gaussian(own_key, extent, width, limit, shards=(), held_as=jnp.bfloat16):
    drawn = jax.random.normal(own_key, extent, jnp.float32) * width
    if len(shards) > 0:
        drawn = block_levels(own_key, extent, shards, -0.22, 0.18) * drawn
    return jnp.clip(drawn, min=-limit, max=limit).astype(held_as)


def setup_inputs(seed: int = 0) -> dict:
    seeds = jax.random.split(jax.random.key(seed), 10)
    return {
        "pipe_field": gaussian(seeds[0], (RUNS, CELLS, C), 1.0, 6.0, ((0, 4), (1, 8))),
        "conv_weight": gaussian(seeds[1], (LAYERS, 3, C, C), (3 * C) ** -0.5, 0.21875),
        "conv_bias": gaussian(seeds[2], (LAYERS, C), 0.5, 3.0, (), jnp.float32),
        "norm_gain": jnp.clip(1.0 + 0.18 * jax.random.normal(seeds[3], (C,), jnp.float32), 0.1, 1.9),
        "query_weight": draw_query_weight(jax.random.fold_in(seeds[9], 71), 0),
        "key_weight": draw_key_weight(jax.random.fold_in(seeds[9], 71), 0),
        "value_weight": gaussian(seeds[6], (C, C), C ** -0.5, 0.375),
        "out_weight": gaussian(seeds[7], (C, C), C ** -0.5, 0.375),
        "upstream": gaussian(seeds[8], (RUNS, CELLS, C), ((RUNS * CELLS) ** -0.5), 0.0234375, ((0, 4), (1, 8))),
    }


def shifted_rows(rows_in, tap_spacing):
    padding = jnp.zeros((rows_in.shape[0], tap_spacing, rows_in.shape[2]), rows_in.dtype)
    lower_rows = jnp.concatenate([padding, rows_in[:, :-tap_spacing]], axis=1)
    upper_rows = jnp.concatenate([rows_in[:, tap_spacing:], padding], axis=1)
    return (lower_rows, upper_rows)

def flatten(values_in):
    return values_in.reshape(-1, values_in.shape[-1])

def three_taps(lower_rows, middle_rows, upper_rows, weights_in):
    running = jnp.dot(flatten(lower_rows), weights_in[0], preferred_element_type=jnp.float32)
    running = running + jnp.dot(flatten(middle_rows), weights_in[1], preferred_element_type=jnp.float32)
    running = running + jnp.dot(flatten(upper_rows), weights_in[2], preferred_element_type=jnp.float32)
    return running.reshape(middle_rows.shape[:-1] + (weights_in.shape[-1],))

def transposed(error_rows, weights_in):
    return lax.dot_general(error_rows, weights_in, (((1,), (1,)), ((), ())), preferred_element_type=jnp.float32)

def outer_sum(input_rows, error_rows):
    return lax.dot_general(input_rows, error_rows, (((0,), (0,)), ((), ())), preferred_element_type=jnp.float32)

def rms_scaled(values_in):
    return values_in * lax.rsqrt(lax.optimization_barrier(jnp.mean(values_in * values_in, axis=-1, keepdims=True)) + 1e-06)

def exact_product(left, right):
    return jnp.dot(left, right.astype(jnp.float32), precision=lax.Precision.HIGHEST, preferred_element_type=jnp.float32)

def attend_run(query_rows, key_rows, value_rows):
    pooled_count = key_rows.shape[0]
    block_rows = min(512, pooled_count)
    head_width = query_rows.shape[1] // HEADS
    key_heads = key_rows.astype(jnp.float32).reshape(pooled_count, HEADS, head_width)
    value_heads = value_rows.astype(jnp.float32).reshape(pooled_count, HEADS, head_width)
    query_blocks = query_rows.reshape(-1, block_rows, query_rows.shape[1])

    def one_block(query_block):
        query_heads = query_block.astype(jnp.float32).reshape(block_rows, HEADS, head_width)
        scores = jnp.einsum('qhd,khd->hqk', query_heads, key_heads, precision=lax.Precision.HIGHEST) * head_width ** (-0.5)
        row_peak = lax.optimization_barrier(jnp.max(scores, axis=-1, keepdims=True))
        exponent = jnp.exp(scores - row_peak)
        denominator = lax.optimization_barrier(jnp.sum(exponent, axis=-1))
        rounded = lax.optimization_barrier(exponent.astype(jnp.bfloat16)).astype(jnp.float32)
        context = jnp.einsum('hqk,khd->hqd', rounded, value_heads, precision=lax.Precision.HIGHEST) / denominator[..., None]
        return jnp.transpose(context, (1, 0, 2)).reshape(block_rows, -1)
    return lax.map(one_block, query_blocks).reshape(pooled_count, -1)

def reference(pipe_field, conv_weight, conv_bias, norm_gain, query_weight, key_weight, value_weight, out_weight, upstream):
    layer_spacings = (FIRST_SPACING, SECOND_SPACING, THIRD_SPACING)
    hidden = pipe_field
    stored = []
    for layer_index in range(LAYERS):
        lower_rows, upper_rows = shifted_rows(hidden, layer_spacings[layer_index])
        preact = three_taps(lower_rows, hidden, upper_rows, conv_weight[layer_index]) + conv_bias[layer_index]
        stored.append((hidden, preact))
        hidden = (hidden.astype(jnp.float32) + jax.nn.silu(preact)).astype(jnp.bfloat16)
    run_count, cell_count, channels = hidden.shape
    pooled = lax.optimization_barrier(jnp.mean(hidden.astype(jnp.float32).reshape(run_count, cell_count // POOL, POOL, channels), axis=2))
    normed = rms_scaled(pooled) * norm_gain
    flat_normed = flatten(normed)
    pooled_shape = pooled.shape
    queries = exact_product(flat_normed, query_weight).reshape(pooled_shape)
    keys_all = exact_product(flat_normed, key_weight).reshape(pooled_shape)
    values_all = exact_product(flat_normed, value_weight).astype(jnp.bfloat16).reshape(pooled_shape)
    contexts = lax.map(lambda triple: attend_run(triple[0], triple[1], triple[2]), (queries, keys_all, values_all))
    context_normed = rms_scaled(contexts).astype(jnp.bfloat16)
    attended = jnp.dot(flatten(context_normed), out_weight, preferred_element_type=jnp.float32).reshape(pooled_shape)
    cotangent = upstream
    weight_parts = [None] * LAYERS
    bias_parts = [None] * LAYERS
    for layer_index in reversed(range(LAYERS)):
        hidden_in, preact = stored[layer_index]
        gate_sig = jax.nn.sigmoid(preact)
        errors = (cotangent.astype(jnp.float32) * gate_sig * (1.0 + preact * (1.0 - gate_sig))).astype(jnp.bfloat16)
        lower_rows, upper_rows = shifted_rows(hidden_in, layer_spacings[layer_index])
        flat_errors = flatten(errors)
        weight_parts[layer_index] = jnp.stack([outer_sum(flatten(lower_rows), flat_errors), outer_sum(flatten(hidden_in), flat_errors), outer_sum(flatten(upper_rows), flat_errors)])
        bias_parts[layer_index] = lax.optimization_barrier(jnp.sum(errors.astype(jnp.float32), axis=(0, 1)))
        if layer_index > 0:
            error_lower, error_upper = shifted_rows(errors, layer_spacings[layer_index])
            back_terms = transposed(flatten(error_upper), conv_weight[layer_index, 0])
            back_terms = back_terms + transposed(flat_errors, conv_weight[layer_index, 1])
            back_terms = back_terms + transposed(flatten(error_lower), conv_weight[layer_index, 2])
            cotangent = (cotangent.astype(jnp.float32) + back_terms.reshape(cotangent.shape)).astype(jnp.bfloat16)
    return (attended, jnp.stack(weight_parts), jnp.stack(bias_parts))
```

```python
import jax
import jax.numpy as jnp
from jax import lax
from jax.sharding import PartitionSpec as P

HEADS = 4
FIRST_SPACING = 2048
SECOND_SPACING = 4096
THIRD_SPACING = 8192
POOL = 8


def shifted(value, axis, steps):
    count = lax.axis_size(axis)
    initial, last = (max(0, -steps), min(count, count - steps))
    return lax.ppermute(value, axis, [(source, source + steps) for source in range(initial, last)])


def neighbours(block_rows, device_hops):
    lower_rows = shifted(block_rows, "seq", device_hops)
    upper_rows = shifted(block_rows, "seq", -device_hops)
    return (lower_rows, upper_rows)


def three_taps(lower_rows, middle_rows, upper_rows, weights_in):
    running = jnp.dot(lower_rows, weights_in[0], preferred_element_type=jnp.float32)
    running = running + jnp.dot(middle_rows, weights_in[1], preferred_element_type=jnp.float32)
    return running + jnp.dot(upper_rows, weights_in[2], preferred_element_type=jnp.float32)


def transposed(error_rows, weights_in):
    return lax.dot_general(
        error_rows, weights_in, (((1,), (1,)), ((), ())), preferred_element_type=jnp.float32
    )


def outer_sum(input_rows, error_rows):
    return lax.dot_general(
        input_rows, error_rows, (((0,), (0,)), ((), ())), preferred_element_type=jnp.float32
    )


def rms_scaled(values_in):
    return values_in * lax.rsqrt(jnp.mean(values_in * values_in, axis=-1, keepdims=True) + 1e-06)


def exact_product(left, right):
    return jnp.dot(
        left,
        right.astype(jnp.float32),
        precision=lax.Precision.HIGHEST,
        preferred_element_type=jnp.float32,
    )


def attend_block(state_tuple, query_heads, key_rows, value_rows, score_scale):
    row_peak, running, context_sum = state_tuple
    head_width = query_heads.shape[2]
    key_heads = key_rows.reshape(-1, HEADS, head_width)
    value_heads = value_rows.reshape(-1, HEADS, head_width)
    scores = (
        jnp.einsum(
            "qhd,khd->hqk",
            query_heads,
            key_heads,
            precision=lax.Precision.HIGHEST,
            preferred_element_type=jnp.float32,
        )
        * score_scale
    )
    new_peak = jnp.maximum(row_peak, jnp.max(scores, axis=-1))
    factor = jnp.exp(row_peak - new_peak)
    exponent = jnp.exp(scores - new_peak[..., None])
    running = running * factor + jnp.sum(exponent, axis=-1)
    block_sum = jnp.einsum(
        "hqk,khd->hqd",
        exponent.astype(jnp.bfloat16),
        value_heads,
        preferred_element_type=jnp.float32,
    )
    return (new_peak, running, context_sum * factor[..., None] + block_sum)


def attend(state_tuple, query_heads, key_rows, value_rows, score_scale):
    key_total = key_rows.shape[0]
    block_rows = 2048
    if block_rows == key_total:
        return attend_block(state_tuple, query_heads, key_rows, value_rows, score_scale)

    def block_step(position, current):
        row_start = position * block_rows
        key_part = lax.dynamic_slice_in_dim(key_rows, row_start, block_rows, 0)
        value_part = lax.dynamic_slice_in_dim(value_rows, row_start, block_rows, 0)
        return attend_block(current, query_heads, key_part, value_part, score_scale)

    return lax.fori_loop(0, key_total // block_rows, block_step, state_tuple)


def blocks_shifted(value, blocks):
    pad = jnp.zeros((abs(blocks),) + value.shape[1:], value.dtype)
    if blocks > 0:
        return jnp.concatenate([pad, value[:-blocks]], axis=0)
    return jnp.concatenate([value[-blocks:], pad], axis=0)


def flat(value):
    return value.reshape(-1, value.shape[-1])


def on_device(
    pipe_field,
    conv_weight,
    conv_bias,
    norm_gain,
    query_weight,
    key_weight,
    value_weight,
    out_weight,
    upstream,
):
    run_count, cell_count, channels = pipe_field.shape
    devices = lax.axis_size("seq")
    me = lax.axis_index("seq")
    part = cell_count // devices

    def swapped(value):
        return lax.all_to_all(
            value.reshape(devices, part, channels), "seq", 0, 0, tiled=True
        )

    hidden = swapped(pipe_field)
    cotangent = swapped(upstream)
    stored = []
    for layer_index, tap_spacing in enumerate((FIRST_SPACING, SECOND_SPACING, THIRD_SPACING)):
        hops = tap_spacing // cell_count
        lower_rows = flat(blocks_shifted(hidden, hops))
        upper_rows = flat(blocks_shifted(hidden, -hops))
        preact = (
            three_taps(lower_rows, flat(hidden), upper_rows, conv_weight[layer_index])
            + conv_bias[layer_index]
        ).reshape(hidden.shape)
        stored.append((hidden, lower_rows, upper_rows, preact, hops))
        hidden = (hidden.astype(jnp.float32) + jax.nn.silu(preact)).astype(jnp.bfloat16)
    pooled = jnp.mean(
        hidden.astype(jnp.float32).reshape(devices, part // POOL, POOL, channels), axis=2
    )
    normed = rms_scaled(pooled) * norm_gain
    head_width = channels // HEADS
    score_scale = head_width ** (-0.5)
    gathered = lax.all_gather(normed, "seq", axis=0)
    mine = lax.dynamic_index_in_dim(gathered, me, 1, keepdims=False)
    pool_rows = cell_count // POOL
    query_heads = exact_product(flat(mine), query_weight).reshape(pool_rows, HEADS, head_width)
    initial = (
        jnp.full((HEADS, pool_rows), -1e30, jnp.float32),
        jnp.zeros((HEADS, pool_rows), jnp.float32),
        jnp.zeros((HEADS, pool_rows, head_width), jnp.float32),
    )
    keys = exact_product(flat(gathered), key_weight).astype(jnp.bfloat16).astype(jnp.float32)
    values = exact_product(flat(gathered), value_weight).astype(jnp.bfloat16)
    final_peak, running, context_sum = attend(initial, query_heads, keys, values, score_scale)
    context = jnp.transpose(context_sum / running[..., None], (1, 0, 2)).reshape(
        pool_rows, channels
    )
    context_normed = rms_scaled(context).astype(jnp.bfloat16)
    attended = jnp.dot(context_normed, out_weight, preferred_element_type=jnp.float32)
    attended = attended.reshape(run_count, pool_rows, channels)
    weight_parts = [None] * len(stored)
    bias_parts = [None] * len(stored)
    for layer_index in reversed(range(len(stored))):
        hidden_in, lower_rows, upper_rows, preact, hops = stored[layer_index]
        gate_sig = jax.nn.sigmoid(preact)
        errors = (
            cotangent.astype(jnp.float32) * gate_sig * (1.0 + preact * (1.0 - gate_sig))
        ).astype(jnp.bfloat16)
        rows = flat(errors)
        weight_parts[layer_index] = jnp.concatenate(
            [
                outer_sum(lower_rows, rows),
                outer_sum(flat(hidden_in), rows),
                outer_sum(upper_rows, rows),
            ]
        )
        bias_parts[layer_index] = jnp.sum(rows.astype(jnp.float32), axis=0, keepdims=True)
        if layer_index > 0:
            back_terms = transposed(flat(blocks_shifted(errors, -hops)), conv_weight[layer_index, 0])
            back_terms = back_terms + transposed(rows, conv_weight[layer_index, 1])
            back_terms = back_terms + transposed(
                flat(blocks_shifted(errors, hops)), conv_weight[layer_index, 2]
            )
            cotangent = (
                cotangent.astype(jnp.float32) + back_terms.reshape(cotangent.shape)
            ).astype(jnp.bfloat16)
    packed = jnp.concatenate(weight_parts + bias_parts)
    packed = lax.psum(packed, ("dp", "seq"))
    bias_rows = len(stored)
    weight_grad = packed[:-bias_rows].reshape(conv_weight.shape)
    return (attended, weight_grad, packed[-bias_rows:])


def solution(mesh):
    return jax.shard_map(
        on_device,
        mesh=mesh,
        in_specs=(P("dp", "seq", None), P(), P(), P(), P(), P(), P(), P(), P("dp", "seq", None)),
        out_specs=(P("dp", "seq", None), P(), P()),
        check_vma=False,
    )
```

```python
import functools

import jax
import jax.numpy as jnp
from jax import lax
from jax.experimental import pallas as pl
from jax.experimental.pallas import tpu as pltpu
from jax.sharding import PartitionSpec as P

HEADS = 4
FIRST_SPACING = 2048
SECOND_SPACING = 4096
THIRD_SPACING = 8192
POOL = 8


def shifted(value, axis, steps):
    count = lax.axis_size(axis)
    initial, last = (max(0, -steps), min(count, count - steps))
    return lax.ppermute(value, axis, [(source, source + steps) for source in range(initial, last)])


def neighbours(block_rows, device_hops):
    lower_rows = shifted(block_rows, "seq", device_hops)
    upper_rows = shifted(block_rows, "seq", -device_hops)
    return (lower_rows, upper_rows)


def three_taps(lower_rows, middle_rows, upper_rows, weights_in):
    running = jnp.dot(lower_rows, weights_in[0], preferred_element_type=jnp.float32)
    running = running + jnp.dot(middle_rows, weights_in[1], preferred_element_type=jnp.float32)
    return running + jnp.dot(upper_rows, weights_in[2], preferred_element_type=jnp.float32)


def transposed(error_rows, weights_in):
    return lax.dot_general(
        error_rows, weights_in, (((1,), (1,)), ((), ())), preferred_element_type=jnp.float32
    )


def outer_sum(input_rows, error_rows):
    return lax.dot_general(
        input_rows, error_rows, (((0,), (0,)), ((), ())), preferred_element_type=jnp.float32
    )


def rms_scaled(values_in):
    return values_in * lax.rsqrt(jnp.mean(values_in * values_in, axis=-1, keepdims=True) + 1e-06)


def exact_product(left, right):
    return jnp.dot(
        left,
        right.astype(jnp.float32),
        precision=lax.Precision.HIGHEST,
        preferred_element_type=jnp.float32,
    )


def attend_block(state_tuple, query_heads, key_rows, value_rows, score_scale):
    row_peak, running, context_sum = state_tuple
    head_width = query_heads.shape[2]
    key_heads = key_rows.reshape(-1, HEADS, head_width)
    value_heads = value_rows.reshape(-1, HEADS, head_width)
    scores = (
        jnp.einsum(
            "qhd,khd->hqk",
            query_heads,
            key_heads,
            precision=lax.Precision.HIGHEST,
            preferred_element_type=jnp.float32,
        )
        * score_scale
    )
    new_peak = jnp.maximum(row_peak, jnp.max(scores, axis=-1))
    factor = jnp.exp(row_peak - new_peak)
    exponent = jnp.exp(scores - new_peak[..., None])
    running = running * factor + jnp.sum(exponent, axis=-1)
    block_sum = jnp.einsum(
        "hqk,khd->hqd",
        exponent.astype(jnp.bfloat16),
        value_heads,
        preferred_element_type=jnp.float32,
    )
    return (new_peak, running, context_sum * factor[..., None] + block_sum)


def attend(state_tuple, query_heads, key_rows, value_rows, score_scale):
    key_total = key_rows.shape[0]
    block_rows = 2048
    if block_rows == key_total:
        return attend_block(state_tuple, query_heads, key_rows, value_rows, score_scale)

    def block_step(position, current):
        row_start = position * block_rows
        key_part = lax.dynamic_slice_in_dim(key_rows, row_start, block_rows, 0)
        value_part = lax.dynamic_slice_in_dim(value_rows, row_start, block_rows, 0)
        return attend_block(current, query_heads, key_part, value_part, score_scale)

    return lax.fori_loop(0, key_total // block_rows, block_step, state_tuple)


def blocks_shifted(value, blocks):
    pad = jnp.zeros((abs(blocks),) + value.shape[1:], value.dtype)
    if blocks > 0:
        return jnp.concatenate([pad, value[:-blocks]], axis=0)
    return jnp.concatenate([value[-blocks:], pad], axis=0)


def flat(value):
    return value.reshape(-1, value.shape[-1])


def on_device(
    pipe_field,
    conv_weight,
    conv_bias,
    norm_gain,
    query_weight,
    key_weight,
    value_weight,
    out_weight,
    upstream,
):
    run_count, cell_count, channels = pipe_field.shape
    devices = lax.axis_size("seq")
    me = lax.axis_index("seq")
    part = cell_count // devices

    def swapped(value):
        return lax.all_to_all(
            value.reshape(devices, part, channels), "seq", 0, 0, tiled=True
        )

    hidden = swapped(pipe_field)
    cotangent = swapped(upstream)
    stored = []
    for layer_index, tap_spacing in enumerate((FIRST_SPACING, SECOND_SPACING, THIRD_SPACING)):
        hops = tap_spacing // cell_count
        lower_rows = flat(blocks_shifted(hidden, hops))
        upper_rows = flat(blocks_shifted(hidden, -hops))
        preact = (
            three_taps(lower_rows, flat(hidden), upper_rows, conv_weight[layer_index])
            + conv_bias[layer_index]
        ).reshape(hidden.shape)
        stored.append((hidden, lower_rows, upper_rows, preact, hops))
        hidden = (hidden.astype(jnp.float32) + jax.nn.silu(preact)).astype(jnp.bfloat16)
    pooled = jnp.mean(
        hidden.astype(jnp.float32).reshape(devices, part // POOL, POOL, channels), axis=2
    )
    normed = rms_scaled(pooled) * norm_gain
    head_width = channels // HEADS
    score_scale = head_width ** (-0.5)
    gathered = lax.all_gather(normed, "seq", axis=0)
    mine = lax.dynamic_index_in_dim(gathered, me, 1, keepdims=False)
    pool_rows = cell_count // POOL
    query_heads = exact_product(flat(mine), query_weight).reshape(pool_rows, HEADS, head_width)
    initial = (
        jnp.full((HEADS, pool_rows), -1e30, jnp.float32),
        jnp.zeros((HEADS, pool_rows), jnp.float32),
        jnp.zeros((HEADS, pool_rows, head_width), jnp.float32),
    )
    keys = exact_product(flat(gathered), key_weight).astype(jnp.bfloat16).astype(jnp.float32)
    values = exact_product(flat(gathered), value_weight).astype(jnp.bfloat16)
    final_peak, running, context_sum = attend(initial, query_heads, keys, values, score_scale)
    context = jnp.transpose(context_sum / running[..., None], (1, 0, 2)).reshape(
        pool_rows, channels
    )
    context_normed = rms_scaled(context).astype(jnp.bfloat16)
    attended = jnp.dot(context_normed, out_weight, preferred_element_type=jnp.float32)
    attended = attended.reshape(run_count, pool_rows, channels)
    weight_parts = [None] * len(stored)
    bias_parts = [None] * len(stored)
    for layer_index in reversed(range(len(stored))):
        hidden_in, lower_rows, upper_rows, preact, hops = stored[layer_index]
        gate_sig = jax.nn.sigmoid(preact)
        errors = (
            cotangent.astype(jnp.float32) * gate_sig * (1.0 + preact * (1.0 - gate_sig))
        ).astype(jnp.bfloat16)
        rows = flat(errors)
        weight_parts[layer_index] = jnp.concatenate(
            [
                outer_sum(lower_rows, rows),
                outer_sum(flat(hidden_in), rows),
                outer_sum(upper_rows, rows),
            ]
        )
        bias_parts[layer_index] = jnp.sum(rows.astype(jnp.float32), axis=0, keepdims=True)
        if layer_index > 0:
            back_terms = transposed(flat(blocks_shifted(errors, -hops)), conv_weight[layer_index, 0])
            back_terms = back_terms + transposed(rows, conv_weight[layer_index, 1])
            back_terms = back_terms + transposed(
                flat(blocks_shifted(errors, hops)), conv_weight[layer_index, 2]
            )
            cotangent = (
                cotangent.astype(jnp.float32) + back_terms.reshape(cotangent.shape)
            ).astype(jnp.bfloat16)
    packed = jnp.concatenate(weight_parts + bias_parts)
    packed = lax.psum(packed, ("dp", "seq"))
    bias_rows = len(stored)
    weight_grad = packed[:-bias_rows].reshape(conv_weight.shape)
    return (attended, weight_grad, packed[-bias_rows:])


BF = jnp.bfloat16
F32 = jnp.float32
MESH = pl.DeviceIdType.MESH


def flipped(bit, wanted):
    return 1 - bit if wanted else bit


def mm(left, right):
    return jnp.dot(left, right, preferred_element_type=F32)


def split_two(value):
    high = value.astype(BF)
    return high, (value - high.astype(F32)).astype(BF)


def fused_kernel(
    nb,
    part,
    hops,
    x_hbm,
    w_ref,
    bias_ref,
    gain_ref,
    wq_ref,
    wk_ref,
    wv_ref,
    wo_ref,
    u_hbm,
    att_ref,
    wg_ref,
    bg_ref,
    *scratch,
):
    (hid, cot, err, pre, nrm, keys, vals, ctx, bsum, qh, ql) = scratch[:11]
    (xs, xr, us, ur, loc, ns, nr) = scratch[11:18]
    reduce_refs = [scratch[18 + 8 * c : 26 + 8 * c] for c in range(3)]
    dp = lax.axis_index("dp")
    me = lax.axis_index("seq")
    xpos, core = dp // 2, dp % 2
    zpos, ypos = me // 2, me % 2
    z1, z0 = zpos // 2, zpos % 2
    channels = x_hbm.shape[-1]
    layers = len(hops)

    def z_peer(k):
        return flipped(z1, k >> 1) * 2 + flipped(z0, k & 1)

    def plane_peer(k):
        return flipped(xpos, k >> 1), flipped(ypos, k & 1)

    def seq_peer(k):
        return z_peer(k >> 1) * 2 + flipped(ypos, k & 1)

    core_id = (xpos * 2 + (1 - core), me)
    plane_ids = [None]
    plane_q = [None]
    for k in range(1, 4):
        px, py = plane_peer(k)
        plane_ids.append((px * 2 + core, zpos * 2 + py))
        plane_q.append(px * 2 + py)
    z_ids = [None] + [(dp, z_peer(k) * 2 + ypos) for k in range(1, 4)]
    seq_ids = [None] + [(dp, seq_peer(k)) for k in range(1, nb)]
    quad = xpos * 2 + ypos

    barrier = pltpu.get_barrier_semaphore()
    greeted = [core_id, plane_ids[2], plane_ids[3]] + seq_ids[1:]
    for ident in greeted:
        pl.semaphore_signal(barrier, inc=1, device_id=ident, device_id_type=MESH)
    pl.semaphore_wait(barrier, len(greeted))

    def remote(src, dst, ssem, rsem, ident):
        return pltpu.make_async_remote_copy(
            src_ref=src, dst_ref=dst, send_sem=ssem, recv_sem=rsem,
            device_id=ident, device_id_type=MESH,
        )

    def exchange(src_hbm, dst, ssem, rsem):
        copies = []
        for k in range(1, nb):
            peer = seq_peer(k)
            copies.append(
                remote(
                    src_hbm.at[0, pl.ds(pl.multiple_of(peer * part, part), part)],
                    dst.at[me], ssem.at[k], rsem.at[k], seq_ids[k],
                )
            )
        return copies

    x_copies = exchange(x_hbm, hid.at[0], xs, xr)
    u_copies = exchange(u_hbm, cot, us, ur)
    for copy in x_copies:
        copy.start()
    own_rows = pl.ds(pl.multiple_of(me * part, part), part)
    x_own = pltpu.make_async_copy(x_hbm.at[0, own_rows], hid.at[0, me], loc.at[0])
    u_own = pltpu.make_async_copy(u_hbm.at[0, own_rows], cot.at[me], loc.at[1])
    x_own.start()
    u_own.start()
    for copy in x_copies:
        copy.wait_send()
    for copy in u_copies:
        copy.start()
    x_own.wait()
    for copy in x_copies:
        copy.wait_recv()

    for layer in range(layers):
        hop = hops[layer]
        for s in range(nb):
            total = mm(hid[layer, s], w_ref[layer, 1]) + bias_ref[layer : layer + 1]
            if s - hop >= 0:
                total = total + mm(hid[layer, s - hop], w_ref[layer, 0])
            if s + hop < nb:
                total = total + mm(hid[layer, s + hop], w_ref[layer, 2])
            pre[layer, s] = total
            active = total / (1.0 + jnp.exp(-total))
            after = (hid[layer, s].astype(F32) + active).astype(BF)
            if layer < layers - 1:
                hid[layer + 1, s] = after
            else:
                pooled = jnp.mean(
                    after.astype(F32).reshape(part // POOL, POOL, channels), axis=1
                )
                nrm[me, s] = rms_scaled(pooled) * gain_ref[...]

    near = remote(nrm.at[me], nrm.at[me], ns.at[0], nr.at[0], z_ids[1])
    far = remote(nrm.at[me], nrm.at[me], ns.at[1], nr.at[1], z_ids[2])
    far.start()
    near.start()
    y_id = (dp, zpos * 2 + (1 - ypos))

    def to_y(k):
        place = nrm.at[z_peer(k) * 2 + ypos]
        return remote(place, place, ns.at[3 + k], nr.at[3 + k], y_id)

    sides = [to_y(k) for k in range(4)]
    sides[0].start()
    near_place = nrm.at[z_peer(2) * 2 + ypos]
    relay = remote(near_place, near_place, ns.at[2], nr.at[2], z_ids[1])
    far.wait_recv()
    relay.start()
    sides[2].start()
    near.wait_recv()
    sides[1].start()

    copies_of = [None] * layers

    def reduce_open(layer):
        own, send, r1, s1, r2, r3, g, other = reduce_refs[layer][:8]
        rows = own.shape[1]
        main = rows if layer else rows - 16
        ssem, rsem = sems_of[layer]
        grad = wg_ref[layer].reshape(-1, channels)
        left, right = grad[:, :128], grad[:, 128:]
        mine = jnp.where(core == 0, left, right).reshape(16, main, 128)
        theirs = jnp.where(core == 0, right, left).reshape(16, main, 128)
        own[:, :main] = mine
        send[:, :main] = theirs.astype(BF)
        if main != rows:
            own[:, main:] = jnp.zeros((16, 16, 128), F32)
            send[:, main:] = jnp.zeros((16, 16, 128), BF)
            low, high = bsum[:, :128], bsum[:, 128:]
            own[0, main:] = jnp.where(core == 0, low, high)
            send[0, main:] = jnp.where(core == 0, high, low).astype(BF)
        first = [remote(send, r1, ssem.at[0], rsem.at[0], core_id)]
        second = [
            remote(
                s1.at[pl.ds(plane_q[k] * 4, 4)], r2.at[k - 1],
                ssem.at[k], rsem.at[k], plane_ids[k],
            )
            for k in range(1, 4)
        ]
        third = [
            remote(
                s1.at[quad * 4 + z_peer(k)], r3.at[k - 1],
                ssem.at[3 + k], rsem.at[3 + k], z_ids[k],
            )
            for k in range(1, 4)
        ]
        mine_at = g.at[quad * 4 + zpos]
        fourth = [
            remote(mine_at, mine_at, ssem.at[6 + k], rsem.at[6 + k], z_ids[k])
            for k in range(1, 4)
        ]
        group = g.at[pl.ds(quad * 4, 4)]
        fifth = [
            remote(group, group, ssem.at[9 + k], rsem.at[9 + k], plane_ids[k])
            for k in range(1, 4)
        ]
        sixth = [remote(g, other, ssem.at[13], rsem.at[13], core_id)]
        copies_of[layer] = [first, second, third, fourth, fifth, sixth]
        for copy in first:
            copy.start()

    def reduce_step(layer, stage):
        own, send, r1, s1, r2, r3, g, other = reduce_refs[layer][:8]
        for copy in copies_of[layer][stage]:
            copy.wait()
        group = pl.ds(quad * 4, 4)
        if stage == 0:
            own[...] = own[...] + r1[...].astype(F32)
            s1[...] = own[...].astype(BF)
        elif stage == 1:
            total = own[group] + r2[0].astype(F32) + r2[1].astype(F32) + r2[2].astype(F32)
            own[group] = total
            s1[group] = total.astype(BF)
        elif stage == 2:
            place = quad * 4 + zpos
            total = own[place] + r3[0].astype(F32) + r3[1].astype(F32) + r3[2].astype(F32)
            g[place] = total.astype(BF)
        elif stage == 5:
            rows = own.shape[1]
            main = rows if layer else rows - 16
            a, b = g[:, :main].astype(F32), other[:, :main].astype(F32)
            low, high = jnp.where(core == 0, a, b), jnp.where(core == 0, b, a)
            wg_ref[layer, :, :, :128] = low.reshape(3, channels, 128)
            wg_ref[layer, :, :, 128:] = high.reshape(3, channels, 128)
            if main != rows:
                a, b = g[0, main:].astype(F32), other[0, main:].astype(F32)
                bg_ref[:, :128] = jnp.where(core == 0, a, b)[:layers]
                bg_ref[:, 128:] = jnp.where(core == 0, b, a)[:layers]
        if stage < 5:
            for copy in copies_of[layer][stage + 1]:
                copy.start()

    sem_refs = scratch[42:]
    sems_of = [(sem_refs[2 * c], sem_refs[2 * c + 1]) for c in range(3)]

    def backward(layer):
        hop = hops[layer]
        width = part
        bias_total = jnp.zeros((1, channels), F32)
        for s in range(nb):
            v = pre[layer, s]
            gate = 1.0 / (1.0 + jnp.exp(-v))
            e = (cot[s].astype(F32) * gate * (1.0 + v * (1.0 - gate))).astype(BF)
            err[s] = e
            bias_total = bias_total + jnp.sum(e.astype(F32), axis=0, keepdims=True)
        bsum[layer : layer + 1] = bias_total

        def outer(first_block, err_block, count):
            rows = hid[layer, first_block : first_block + count].reshape(count * width, channels)
            errs = err[err_block : err_block + count].reshape(count * width, channels)
            return outer_sum(rows, errs)

        wg_ref[layer, 0] = outer(0, hop, nb - hop)
        wg_ref[layer, 1] = outer(0, 0, nb)
        wg_ref[layer, 2] = outer(hop, 0, nb - hop)
        reduce_open(layer)
        if layer == 0:
            return
        for s in range(nb):
            total = cot[s].astype(F32) + transposed(err[s], w_ref[layer, 1])
            if s + hop < nb:
                total = total + transposed(err[s + hop], w_ref[layer, 0])
            if s - hop >= 0:
                total = total + transposed(err[s - hop], w_ref[layer, 2])
            cot[s] = total.astype(BF)

    bsum[...] = jnp.zeros(bsum.shape, F32)
    u_own.wait()
    for copy in u_copies:
        copy.wait()
    backward(2)
    relay.wait_recv()
    sides[3].start()
    backward(1)
    reduce_step(2, 0)
    backward(0)
    reduce_step(1, 0)
    reduce_step(2, 1)

    for copy in sides:
        copy.wait_recv()
    head_width = channels // HEADS
    per = part // POOL
    mine = nrm[:, pl.ds(me, 1)].reshape(nb * per, channels)
    high, low = split_two(mine)
    q = (mm(high, wq_ref[...]) + mm(low, wq_ref[...])) * head_width ** (-0.5)
    q_high, q_low = split_two(q)
    qh[...] = q_high
    ql[...] = q_low
    for d in range(nb):
        high, low = split_two(nrm[d].reshape(nb * per, channels))
        rows = slice(d * nb * per, (d + 1) * nb * per)
        keys[rows] = (mm(high, wk_ref[...]) + mm(low, wk_ref[...])).astype(BF)
        vals[rows] = (mm(high, wv_ref[...]) + mm(low, wv_ref[...])).astype(BF)
    reduce_step(0, 0)
    reduce_step(1, 1)
    reduce_step(2, 2)

    for head in range(HEADS):
        lanes = slice(head * head_width, (head + 1) * head_width)
        scores = transposed(qh[:, lanes], keys[:, lanes]) + transposed(ql[:, lanes], keys[:, lanes])
        peak = jnp.max(scores, axis=-1, keepdims=True)
        expo = jnp.exp(scores - peak)
        den = jnp.sum(expo, axis=-1, keepdims=True)
        ctx[:, lanes] = mm(expo.astype(BF), vals[:, lanes]) / den
        reduce_step(0, 1 + head)
        if head < 3:
            reduce_step(1, 2 + head)
        if head < 3:
            reduce_step(2, 3 + head)
        if head == 3:
            reduce_step(1, 5)
    att_ref[0] = mm(rms_scaled(ctx[...]).astype(BF), wo_ref[...])
    reduce_step(0, 5)
    for copy in [near, far, relay] + sides:
        copy.wait_send()


def fused(mesh, *args):
    pipe_field, conv_weight = args[0], args[1]
    cells, channels = pipe_field.shape[1:]
    nb = mesh.shape["seq"]
    part = cells // nb
    layers = conv_weight.shape[0]
    hops = tuple(h // cells for h in (FIRST_SPACING, SECOND_SPACING, THIRD_SPACING))
    pool_rows = cells // POOL
    per = part // POOL
    dma = pltpu.SemaphoreType.DMA
    vm = pltpu.VMEM
    scratch = [
        vm((layers, nb, part, channels), BF),
        vm((nb, part, channels), BF),
        vm((nb, part, channels), BF),
        vm((layers, nb, part, channels), F32),
        vm((nb, nb, per, channels), F32),
        vm((nb * pool_rows, channels), BF),
        vm((nb * pool_rows, channels), BF),
        vm((pool_rows, channels), F32),
        vm((16, channels), F32),
        vm((pool_rows, channels), BF),
        vm((pool_rows, channels), BF),
        dma((nb,)), dma((nb,)), dma((nb,)), dma((nb,)), dma((2,)), dma((7,)), dma((7,)),
    ]
    for layer in range(layers):
        rows = 3 * channels // 16 + (0 if layer else 16)
        scratch += [
            vm((16, rows, 128), F32),
            vm((16, rows, 128), BF),
            vm((16, rows, 128), BF),
            vm((16, rows, 128), BF),
            vm((3, 4, rows, 128), BF),
            vm((3, rows, 128), BF),
            vm((16, rows, 128), BF),
            vm((16, rows, 128), BF),
        ]
    for layer in range(layers):
        scratch += [dma((14,)), dma((14,))]
    inner = pl.BlockSpec(memory_space=pltpu.VMEM)
    outer = pl.BlockSpec(memory_space=pl.ANY)
    gain = args[3].reshape(1, channels)
    return pl.pallas_call(
        functools.partial(fused_kernel, nb, part, hops),
        out_shape=(
            jax.ShapeDtypeStruct((1, pool_rows, channels), F32),
            jax.ShapeDtypeStruct(conv_weight.shape, F32),
            jax.ShapeDtypeStruct((layers, channels), F32),
        ),
        in_specs=[outer] + [inner] * 7 + [outer],
        out_specs=(inner, inner, inner),
        scratch_shapes=scratch,
        compiler_params=pltpu.CompilerParams(
            collective_id=0, has_side_effects=True, vmem_limit_bytes=50 * 1024 * 1024
        ),
        cost_estimate=pl.CostEstimate(
            flops=9 * 10**9, bytes_accessed=8 * 10**6, transcendentals=6 * 10**6
        ),
    )(pipe_field, conv_weight, args[2], gain, *args[4:])


def solution(mesh):
    small = mesh.shape["seq"] == 8 and mesh.shape["dp"] == 4
    return jax.shard_map(
        functools.partial(fused, mesh) if small else on_device,
        mesh=mesh,
        in_specs=(P("dp", "seq", None), P(), P(), P(), P(), P(), P(), P(), P("dp", "seq", None)),
        out_specs=(P("dp", "seq", None), P(), P()),
        check_vma=False,
    )
```

```python
import functools

import jax
import jax.numpy as jnp
from jax import lax
from jax.experimental import pallas as pl
from jax.experimental.pallas import tpu as pltpu
from jax.sharding import PartitionSpec as P

HEADS = 4
FIRST_SPACING = 2048
SECOND_SPACING = 4096
THIRD_SPACING = 8192
POOL = 8


def shifted(value, axis, steps):
    count = lax.axis_size(axis)
    initial, last = (max(0, -steps), min(count, count - steps))
    return lax.ppermute(value, axis, [(source, source + steps) for source in range(initial, last)])


def neighbours(block_rows, device_hops):
    lower_rows = shifted(block_rows, "seq", device_hops)
    upper_rows = shifted(block_rows, "seq", -device_hops)
    return (lower_rows, upper_rows)


def three_taps(lower_rows, middle_rows, upper_rows, weights_in):
    running = jnp.dot(lower_rows, weights_in[0], preferred_element_type=jnp.float32)
    running = running + jnp.dot(middle_rows, weights_in[1], preferred_element_type=jnp.float32)
    return running + jnp.dot(upper_rows, weights_in[2], preferred_element_type=jnp.float32)


def transposed(error_rows, weights_in):
    return lax.dot_general(
        error_rows, weights_in, (((1,), (1,)), ((), ())), preferred_element_type=jnp.float32
    )


def outer_sum(input_rows, error_rows):
    return lax.dot_general(
        input_rows, error_rows, (((0,), (0,)), ((), ())), preferred_element_type=jnp.float32
    )


def rms_scaled(values_in):
    return values_in * lax.rsqrt(jnp.mean(values_in * values_in, axis=-1, keepdims=True) + 1e-06)


def exact_product(left, right):
    return jnp.dot(
        left,
        right.astype(jnp.float32),
        precision=lax.Precision.HIGHEST,
        preferred_element_type=jnp.float32,
    )


def attend_block(state_tuple, query_heads, key_rows, value_rows, score_scale):
    row_peak, running, context_sum = state_tuple
    head_width = query_heads.shape[2]
    key_heads = key_rows.reshape(-1, HEADS, head_width)
    value_heads = value_rows.reshape(-1, HEADS, head_width)
    scores = (
        jnp.einsum(
            "qhd,khd->hqk",
            query_heads,
            key_heads,
            precision=lax.Precision.HIGHEST,
            preferred_element_type=jnp.float32,
        )
        * score_scale
    )
    new_peak = jnp.maximum(row_peak, jnp.max(scores, axis=-1))
    factor = jnp.exp(row_peak - new_peak)
    exponent = jnp.exp(scores - new_peak[..., None])
    running = running * factor + jnp.sum(exponent, axis=-1)
    block_sum = jnp.einsum(
        "hqk,khd->hqd",
        exponent.astype(jnp.bfloat16),
        value_heads,
        preferred_element_type=jnp.float32,
    )
    return (new_peak, running, context_sum * factor[..., None] + block_sum)


def attend(state_tuple, query_heads, key_rows, value_rows, score_scale):
    key_total = key_rows.shape[0]
    block_rows = 2048
    if block_rows == key_total:
        return attend_block(state_tuple, query_heads, key_rows, value_rows, score_scale)

    def block_step(position, current):
        row_start = position * block_rows
        key_part = lax.dynamic_slice_in_dim(key_rows, row_start, block_rows, 0)
        value_part = lax.dynamic_slice_in_dim(value_rows, row_start, block_rows, 0)
        return attend_block(current, query_heads, key_part, value_part, score_scale)

    return lax.fori_loop(0, key_total // block_rows, block_step, state_tuple)


def blocks_shifted(value, blocks):
    pad = jnp.zeros((abs(blocks),) + value.shape[1:], value.dtype)
    if blocks > 0:
        return jnp.concatenate([pad, value[:-blocks]], axis=0)
    return jnp.concatenate([value[-blocks:], pad], axis=0)


def flat(value):
    return value.reshape(-1, value.shape[-1])


def on_device(
    pipe_field,
    conv_weight,
    conv_bias,
    norm_gain,
    query_weight,
    key_weight,
    value_weight,
    out_weight,
    upstream,
):
    run_count, cell_count, channels = pipe_field.shape
    devices = lax.axis_size("seq")
    me = lax.axis_index("seq")
    part = cell_count // devices

    def swapped(value):
        return lax.all_to_all(
            value.reshape(devices, part, channels), "seq", 0, 0, tiled=True
        )

    hidden = swapped(pipe_field)
    cotangent = swapped(upstream)
    stored = []
    for layer_index, tap_spacing in enumerate((FIRST_SPACING, SECOND_SPACING, THIRD_SPACING)):
        hops = tap_spacing // cell_count
        lower_rows = flat(blocks_shifted(hidden, hops))
        upper_rows = flat(blocks_shifted(hidden, -hops))
        preact = (
            three_taps(lower_rows, flat(hidden), upper_rows, conv_weight[layer_index])
            + conv_bias[layer_index]
        ).reshape(hidden.shape)
        stored.append((hidden, lower_rows, upper_rows, preact, hops))
        hidden = (hidden.astype(jnp.float32) + jax.nn.silu(preact)).astype(jnp.bfloat16)
    pooled = jnp.mean(
        hidden.astype(jnp.float32).reshape(devices, part // POOL, POOL, channels), axis=2
    )
    normed = rms_scaled(pooled) * norm_gain
    head_width = channels // HEADS
    score_scale = head_width ** (-0.5)
    gathered = lax.all_gather(normed, "seq", axis=0)
    mine = lax.dynamic_index_in_dim(gathered, me, 1, keepdims=False)
    pool_rows = cell_count // POOL
    query_heads = exact_product(flat(mine), query_weight).reshape(pool_rows, HEADS, head_width)
    initial = (
        jnp.full((HEADS, pool_rows), -1e30, jnp.float32),
        jnp.zeros((HEADS, pool_rows), jnp.float32),
        jnp.zeros((HEADS, pool_rows, head_width), jnp.float32),
    )
    keys = exact_product(flat(gathered), key_weight).astype(jnp.bfloat16).astype(jnp.float32)
    values = exact_product(flat(gathered), value_weight).astype(jnp.bfloat16)
    final_peak, running, context_sum = attend(initial, query_heads, keys, values, score_scale)
    context = jnp.transpose(context_sum / running[..., None], (1, 0, 2)).reshape(
        pool_rows, channels
    )
    context_normed = rms_scaled(context).astype(jnp.bfloat16)
    attended = jnp.dot(context_normed, out_weight, preferred_element_type=jnp.float32)
    attended = attended.reshape(run_count, pool_rows, channels)
    weight_parts = [None] * len(stored)
    bias_parts = [None] * len(stored)
    for layer_index in reversed(range(len(stored))):
        hidden_in, lower_rows, upper_rows, preact, hops = stored[layer_index]
        gate_sig = jax.nn.sigmoid(preact)
        errors = (
            cotangent.astype(jnp.float32) * gate_sig * (1.0 + preact * (1.0 - gate_sig))
        ).astype(jnp.bfloat16)
        rows = flat(errors)
        weight_parts[layer_index] = jnp.concatenate(
            [
                outer_sum(lower_rows, rows),
                outer_sum(flat(hidden_in), rows),
                outer_sum(upper_rows, rows),
            ]
        )
        bias_parts[layer_index] = jnp.sum(rows.astype(jnp.float32), axis=0, keepdims=True)
        if layer_index > 0:
            back_terms = transposed(flat(blocks_shifted(errors, -hops)), conv_weight[layer_index, 0])
            back_terms = back_terms + transposed(rows, conv_weight[layer_index, 1])
            back_terms = back_terms + transposed(
                flat(blocks_shifted(errors, hops)), conv_weight[layer_index, 2]
            )
            cotangent = (
                cotangent.astype(jnp.float32) + back_terms.reshape(cotangent.shape)
            ).astype(jnp.bfloat16)
    packed = jnp.concatenate(weight_parts + bias_parts)
    packed = lax.psum(packed, ("dp", "seq"))
    bias_rows = len(stored)
    weight_grad = packed[:-bias_rows].reshape(conv_weight.shape)
    return (attended, weight_grad, packed[-bias_rows:])


BF = jnp.bfloat16
F32 = jnp.float32
MESH = pl.DeviceIdType.MESH


def flipped(bit, wanted):
    return 1 - bit if wanted else bit


def mm(left, right):
    return jnp.dot(left, right, preferred_element_type=F32)


def split_two(value):
    high = value.astype(BF)
    return high, (value - high.astype(F32)).astype(BF)


def fused_kernel(
    nb,
    part,
    hops,
    x_hbm,
    w_ref,
    bias_ref,
    gain_ref,
    wq_ref,
    wk_ref,
    wv_ref,
    wo_ref,
    u_hbm,
    att_ref,
    wg_ref,
    bg_ref,
    *scratch,
):
    (hid, cot, err, pre, nrm, keys, vals, ctx, bsum, qh, ql) = scratch[:11]
    (xs, xr, us, ur, loc, ns, nr) = scratch[11:18]
    reduce_refs = [scratch[18 + 8 * c : 26 + 8 * c] for c in range(3)]
    dp = lax.axis_index("dp")
    me = lax.axis_index("seq")
    xpos, core = dp // 2, dp % 2
    zpos, ypos = me // 2, me % 2
    z1, z0 = zpos // 2, zpos % 2
    channels = x_hbm.shape[-1]
    layers = len(hops)

    def z_peer(k):
        return flipped(z1, k >> 1) * 2 + flipped(z0, k & 1)

    def plane_peer(k):
        return flipped(xpos, k >> 1), flipped(ypos, k & 1)

    def seq_peer(k):
        return z_peer(k >> 1) * 2 + flipped(ypos, k & 1)

    core_id = (xpos * 2 + (1 - core), me)
    plane_ids = [None]
    plane_q = [None]
    for k in range(1, 4):
        px, py = plane_peer(k)
        plane_ids.append((px * 2 + core, zpos * 2 + py))
        plane_q.append(px * 2 + py)
    z_ids = [None] + [(dp, z_peer(k) * 2 + ypos) for k in range(1, 4)]
    seq_ids = [None] + [(dp, seq_peer(k)) for k in range(1, nb)]
    quad = xpos * 2 + ypos

    barrier = pltpu.get_barrier_semaphore()
    greeted = [core_id, plane_ids[2], plane_ids[3]] + seq_ids[1:]
    for ident in greeted:
        pl.semaphore_signal(barrier, inc=1, device_id=ident, device_id_type=MESH)
    pl.semaphore_wait(barrier, len(greeted))

    def remote(src, dst, ssem, rsem, ident):
        return pltpu.make_async_remote_copy(
            src_ref=src, dst_ref=dst, send_sem=ssem, recv_sem=rsem,
            device_id=ident, device_id_type=MESH,
        )

    def exchange(src_hbm, dst, ssem, rsem):
        copies = []
        for k in range(1, nb):
            peer = seq_peer(k)
            copies.append(
                remote(
                    src_hbm.at[0, pl.ds(pl.multiple_of(peer * part, part), part)],
                    dst.at[me], ssem.at[k], rsem.at[k], seq_ids[k],
                )
            )
        return copies

    x_copies = exchange(x_hbm, hid.at[0], xs, xr)
    u_copies = exchange(u_hbm, cot, us, ur)
    for copy in x_copies:
        copy.start()
    own_rows = pl.ds(pl.multiple_of(me * part, part), part)
    x_own = pltpu.make_async_copy(x_hbm.at[0, own_rows], hid.at[0, me], loc.at[0])
    u_own = pltpu.make_async_copy(u_hbm.at[0, own_rows], cot.at[me], loc.at[1])
    x_own.start()
    u_own.start()
    for copy in x_copies:
        copy.wait_send()
    for copy in u_copies:
        copy.start()
    x_own.wait()
    for copy in x_copies:
        copy.wait_recv()

    for layer in range(layers):
        hop = hops[layer]
        for s in range(nb):
            total = mm(hid[layer, s], w_ref[layer, 1]) + bias_ref[layer : layer + 1]
            if s - hop >= 0:
                total = total + mm(hid[layer, s - hop], w_ref[layer, 0])
            if s + hop < nb:
                total = total + mm(hid[layer, s + hop], w_ref[layer, 2])
            pre[layer, s] = total
            active = total * (0.5 + 0.5 * jnp.tanh(0.5 * total))
            after = (hid[layer, s].astype(F32) + active).astype(BF)
            if layer < layers - 1:
                hid[layer + 1, s] = after
            else:
                pooled = jnp.mean(
                    after.astype(F32).reshape(part // POOL, POOL, channels), axis=1
                )
                nrm[me, s] = rms_scaled(pooled) * gain_ref[...]

    near = remote(nrm.at[me], nrm.at[me], ns.at[0], nr.at[0], z_ids[1])
    far = remote(nrm.at[me], nrm.at[me], ns.at[1], nr.at[1], z_ids[2])
    far.start()
    near.start()
    y_id = (dp, zpos * 2 + (1 - ypos))

    def to_y(k):
        place = nrm.at[z_peer(k) * 2 + ypos]
        return remote(place, place, ns.at[3 + k], nr.at[3 + k], y_id)

    sides = [to_y(k) for k in range(4)]
    sides[0].start()
    near_place = nrm.at[z_peer(2) * 2 + ypos]
    relay = remote(near_place, near_place, ns.at[2], nr.at[2], z_ids[1])
    far.wait_recv()
    relay.start()
    sides[2].start()
    near.wait_recv()
    sides[1].start()

    copies_of = [None] * layers

    def reduce_open(layer):
        own, send, r1, s1, r2, r3, g, other = reduce_refs[layer][:8]
        rows = own.shape[1]
        main = rows if layer else rows - 16
        ssem, rsem = sems_of[layer]
        grad = wg_ref[layer].reshape(-1, channels)
        left, right = grad[:, :128], grad[:, 128:]
        mine = jnp.where(core == 0, left, right).reshape(16, main, 128)
        theirs = jnp.where(core == 0, right, left).reshape(16, main, 128)
        own[:, :main] = mine
        send[:, :main] = theirs.astype(BF)
        if main != rows:
            own[:, main:] = jnp.zeros((16, 16, 128), F32)
            send[:, main:] = jnp.zeros((16, 16, 128), BF)
            low, high = bsum[:, :128], bsum[:, 128:]
            own[0, main:] = jnp.where(core == 0, low, high)
            send[0, main:] = jnp.where(core == 0, high, low).astype(BF)
        first = [remote(send, r1, ssem.at[0], rsem.at[0], core_id)]
        second = [
            remote(
                s1.at[pl.ds(plane_q[k] * 4, 4)], r2.at[k - 1],
                ssem.at[k], rsem.at[k], plane_ids[k],
            )
            for k in range(1, 4)
        ]
        third = [
            remote(
                s1.at[quad * 4 + z_peer(k)], r3.at[k - 1],
                ssem.at[3 + k], rsem.at[3 + k], z_ids[k],
            )
            for k in range(1, 4)
        ]
        mine_at = g.at[quad * 4 + zpos]
        fourth = [
            remote(mine_at, mine_at, ssem.at[6 + k], rsem.at[6 + k], z_ids[k])
            for k in range(1, 4)
        ]
        group = g.at[pl.ds(quad * 4, 4)]
        fifth = [
            remote(group, group, ssem.at[9 + k], rsem.at[9 + k], plane_ids[k])
            for k in range(1, 4)
        ]
        sixth = [remote(g, other, ssem.at[13], rsem.at[13], core_id)]
        copies_of[layer] = [first, second, third, fourth, fifth, sixth]
        for copy in first:
            copy.start()

    def reduce_step(layer, stage):
        own, send, r1, s1, r2, r3, g, other = reduce_refs[layer][:8]
        for copy in copies_of[layer][stage]:
            copy.wait()
        group = pl.ds(quad * 4, 4)
        if stage == 0:
            own[...] = own[...] + r1[...].astype(F32)
            s1[...] = own[...].astype(BF)
        elif stage == 1:
            total = own[group] + r2[0].astype(F32) + r2[1].astype(F32) + r2[2].astype(F32)
            own[group] = total
            s1[group] = total.astype(BF)
        elif stage == 2:
            place = quad * 4 + zpos
            total = own[place] + r3[0].astype(F32) + r3[1].astype(F32) + r3[2].astype(F32)
            g[place] = total.astype(BF)
        elif stage == 5:
            rows = own.shape[1]
            main = rows if layer else rows - 16
            a, b = g[:, :main].astype(F32), other[:, :main].astype(F32)
            low, high = jnp.where(core == 0, a, b), jnp.where(core == 0, b, a)
            wg_ref[layer, :, :, :128] = low.reshape(3, channels, 128)
            wg_ref[layer, :, :, 128:] = high.reshape(3, channels, 128)
            if main != rows:
                a, b = g[0, main:].astype(F32), other[0, main:].astype(F32)
                bg_ref[:, :128] = jnp.where(core == 0, a, b)[:layers]
                bg_ref[:, 128:] = jnp.where(core == 0, b, a)[:layers]
        if stage < 5:
            for copy in copies_of[layer][stage + 1]:
                copy.start()

    sem_refs = scratch[42:]
    sems_of = [(sem_refs[2 * c], sem_refs[2 * c + 1]) for c in range(3)]

    def backward(layer):
        hop = hops[layer]
        width = part
        bias_total = jnp.zeros((1, channels), F32)
        for s in range(nb):
            v = pre[layer, s]
            gate = 0.5 + 0.5 * jnp.tanh(0.5 * v)
            e = (cot[s].astype(F32) * gate * (1.0 + v * (1.0 - gate))).astype(BF)
            err[s] = e
            bias_total = bias_total + jnp.sum(e.astype(F32), axis=0, keepdims=True)
        bsum[layer : layer + 1] = bias_total

        def outer(first_block, err_block, count):
            rows = hid[layer, first_block : first_block + count].reshape(count * width, channels)
            errs = err[err_block : err_block + count].reshape(count * width, channels)
            return outer_sum(rows, errs)

        wg_ref[layer, 0] = outer(0, hop, nb - hop)
        wg_ref[layer, 1] = outer(0, 0, nb)
        wg_ref[layer, 2] = outer(hop, 0, nb - hop)
        reduce_open(layer)
        if layer == 0:
            return
        for s in range(nb):
            total = cot[s].astype(F32) + transposed(err[s], w_ref[layer, 1])
            if s + hop < nb:
                total = total + transposed(err[s + hop], w_ref[layer, 0])
            if s - hop >= 0:
                total = total + transposed(err[s - hop], w_ref[layer, 2])
            cot[s] = total.astype(BF)

    bsum[...] = jnp.zeros(bsum.shape, F32)
    u_own.wait()
    for copy in u_copies:
        copy.wait()
    backward(2)
    relay.wait_recv()
    sides[3].start()
    backward(1)
    reduce_step(2, 0)
    backward(0)
    reduce_step(1, 0)
    reduce_step(2, 1)

    for copy in sides:
        copy.wait_recv()
    head_width = channels // HEADS
    per = part // POOL
    mine = nrm[:, pl.ds(me, 1)].reshape(nb * per, channels)
    high, low = split_two(mine)
    q = (mm(high, wq_ref[...]) + mm(low, wq_ref[...])) * head_width ** (-0.5)
    q_high, q_low = split_two(q)
    qh[...] = q_high
    ql[...] = q_low
    for d in range(nb):
        high, low = split_two(nrm[d].reshape(nb * per, channels))
        rows = slice(d * nb * per, (d + 1) * nb * per)
        keys[rows] = (mm(high, wk_ref[...]) + mm(low, wk_ref[...])).astype(BF)
        vals[rows] = (mm(high, wv_ref[...]) + mm(low, wv_ref[...])).astype(BF)
    reduce_step(0, 0)
    reduce_step(1, 1)
    reduce_step(2, 2)

    for head in range(HEADS):
        lanes = slice(head * head_width, (head + 1) * head_width)
        scores = transposed(qh[:, lanes], keys[:, lanes]) + transposed(ql[:, lanes], keys[:, lanes])
        peak = jnp.max(scores, axis=-1, keepdims=True)
        expo = jnp.exp(scores - peak)
        den = jnp.sum(expo, axis=-1, keepdims=True)
        ctx[:, lanes] = mm(expo.astype(BF), vals[:, lanes]) / den
        reduce_step(0, 1 + head)
        if head < 3:
            reduce_step(1, 2 + head)
        if head < 3:
            reduce_step(2, 3 + head)
        if head == 3:
            reduce_step(1, 5)
    att_ref[0] = mm(rms_scaled(ctx[...]).astype(BF), wo_ref[...])
    reduce_step(0, 5)
    for copy in [near, far, relay] + sides:
        copy.wait_send()


def fused(mesh, *args):
    pipe_field, conv_weight = args[0], args[1]
    cells, channels = pipe_field.shape[1:]
    nb = mesh.shape["seq"]
    part = cells // nb
    layers = conv_weight.shape[0]
    hops = tuple(h // cells for h in (FIRST_SPACING, SECOND_SPACING, THIRD_SPACING))
    pool_rows = cells // POOL
    per = part // POOL
    dma = pltpu.SemaphoreType.DMA
    vm = pltpu.VMEM
    scratch = [
        vm((layers, nb, part, channels), BF),
        vm((nb, part, channels), BF),
        vm((nb, part, channels), BF),
        vm((layers, nb, part, channels), F32),
        vm((nb, nb, per, channels), F32),
        vm((nb * pool_rows, channels), BF),
        vm((nb * pool_rows, channels), BF),
        vm((pool_rows, channels), F32),
        vm((16, channels), F32),
        vm((pool_rows, channels), BF),
        vm((pool_rows, channels), BF),
        dma((nb,)), dma((nb,)), dma((nb,)), dma((nb,)), dma((2,)), dma((7,)), dma((7,)),
    ]
    for layer in range(layers):
        rows = 3 * channels // 16 + (0 if layer else 16)
        scratch += [
            vm((16, rows, 128), F32),
            vm((16, rows, 128), BF),
            vm((16, rows, 128), BF),
            vm((16, rows, 128), BF),
            vm((3, 4, rows, 128), BF),
            vm((3, rows, 128), BF),
            vm((16, rows, 128), BF),
            vm((16, rows, 128), BF),
        ]
    for layer in range(layers):
        scratch += [dma((14,)), dma((14,))]
    inner = pl.BlockSpec(memory_space=pltpu.VMEM)
    outer = pl.BlockSpec(memory_space=pl.ANY)
    gain = args[3].reshape(1, channels)
    return pl.pallas_call(
        functools.partial(fused_kernel, nb, part, hops),
        out_shape=(
            jax.ShapeDtypeStruct((1, pool_rows, channels), F32),
            jax.ShapeDtypeStruct(conv_weight.shape, F32),
            jax.ShapeDtypeStruct((layers, channels), F32),
        ),
        in_specs=[outer] + [inner] * 7 + [outer],
        out_specs=(inner, inner, inner),
        scratch_shapes=scratch,
        compiler_params=pltpu.CompilerParams(
            collective_id=0, has_side_effects=True, vmem_limit_bytes=61 * 1024 * 1024
        ),
        cost_estimate=pl.CostEstimate(
            flops=9 * 10**9, bytes_accessed=8 * 10**6, transcendentals=6 * 10**6
        ),
    )(pipe_field, conv_weight, args[2], gain, *args[4:])


def solution(mesh):
    small = mesh.shape["seq"] == 8 and mesh.shape["dp"] == 4
    return jax.shard_map(
        functools.partial(fused, mesh) if small else on_device,
        mesh=mesh,
        in_specs=(P("dp", "seq", None), P(), P(), P(), P(), P(), P(), P(), P("dp", "seq", None)),
        out_specs=(P("dp", "seq", None), P(), P()),
        check_vma=False,
    )
```
